768 devices in a mesh: dp: 24 (over z, x_lo), blk: 16 (over x_hi, y), tensor: 2 (over core).
Axes of the slice: x: 4 (x_hi: 2, x_lo: 2; x = x_hi * 2 + x_lo), y: 8, z: 12, core: 2. Of those that a mesh axis runs over, the one named last changes fastest.
Arguments:
- activations: bfloat16 [98304, 8192], P(('dp', 'blk')), may hold values from -6 to 6
- norm_gain: float32 [8192], replicated, may hold values from 0.5 to 1.5
- key_weight: bfloat16 [8192, 512], P('blk', 'tensor'), may hold values from -0.0625 to 0.0625
- key_grad: bfloat16 [98304, 512], P(('dp', 'blk'), 'tensor'), may hold values from -6 to 6
- doc_lengths: int32 [384, 4], P(('dp', 'blk')), may hold values from 1 to 128, 256 in all within a row
Outputs:
- weight_grad: float32 [8192, 512], P('blk', 'tensor')
- normed_grad: bfloat16 [98304, 8192], P(('dp', 'blk'), 'tensor')
The draws below stay inside these ranges and needn't reach their ends.
Inputs may be any that keep to these rules, and one draw needn't show every extreme that they name: `doc_lengths`: each row sums to 256, and its longest document has exactly 128 tokens.
All inputs are finite; a program needn't handle non-finite values.
Results may differ from the reference program's by a relative error of at most 0.0057.
Values may be sent and summed in bfloat16 or wider, within the bound.
No kernel may reach another device: no remote copies, remote signals or barrier semaphores. Data moves between devices by JAX's collectives and lax.ppermute only.
A program may use at most 64 MiB of HBM per device.

```python
import math
import jax
import jax.numpy as jnp
import numpy as np
from jax import lax

D = 8192
KVH = 4
HS = 128
DOCS = 4
TOK_DEV = 256
MICRO = 384
TOKENS = 98304
KV = 512
N_DP = 24
N_TENSOR = 2


def block_scale(stream_key, dims, split, smallest, largest):
    gain = 1.0
    for position, blocks in split:
        heights = jax.random.uniform(jax.random.fold_in(jax.random.fold_in(stream_key, 6), position), (blocks,), jnp.float32, smallest / len(split), largest / len(split))
        gain = gain * jnp.repeat(jnp.exp(heights), dims[position] // blocks).reshape((-1,) + (1,) * (len(dims) - 1 - position))
    return gain


def profile(count, total, limit, lean):
    weights = [(1 << 20) // math.isqrt(rank ** lean) + 1 for rank in range(2, count + 1)]
    spare, holding = total - limit - (count - 1), [1] * (count - 1)
    while spare > 0:
        movable = [i for i in range(count - 1) if holding[i] < limit]
        mass, left = sum([weights[i] for i in movable]), spare
        for i in movable:
            extra = min(limit - holding[i], max(1, left * weights[i] // mass), spare)
            holding[i] = holding[i] + extra
            spare = spare - extra
    return np.array([limit] + holding)


def uneven_parts(rng, number_of, total, limit, slope):
    if number_of == 2:
        one = jax.random.randint(rng, (), max(1, total - limit), min(limit, total - 1) + 1)
        return jnp.stack([one, total - one])
    tallies = jnp.asarray(profile(number_of, total, limit, slope), jnp.int32)
    twos = (number_of - 1) // 2
    donor, receiver = tallies[1:1 + 2 * twos:2], tallies[2:2 + 2 * twos:2]
    room = jnp.minimum(donor - 1, limit - receiver)
    passed = jax.random.randint(jax.random.fold_in(rng, 1), (twos,), 0, 1 << 20) % (room + 1)
    tallies = tallies.at[1:1 + 2 * twos:2].set(donor - passed).at[2:2 + 2 * twos:2].set(receiver + passed)
    return tallies[jax.random.permutation(jax.random.fold_in(rng, 2), number_of)]


def scatter_about(stream_key, extent, deviation, reach, shards=(), kind=jnp.bfloat16):
    drawn = jax.random.normal(stream_key, extent, jnp.float32) * deviation
    if len(shards) > 0:
        drawn = block_scale(stream_key, extent, shards, -0.22, 0.18) * drawn
    return jnp.clip(drawn, min=-reach, max=reach).astype(kind)


def setup_inputs(seed: int = 0) -> dict:
    key_of = jax.random.split(jax.random.key(seed), 6)
    activations = scatter_about(key_of[0], (TOKENS, D), 1.0, 6.0, ((0, 384),))
    norm_gain = jnp.clip(1.0 + 0.1 * jax.random.normal(key_of[1], (D,), jnp.float32), 0.5, 1.5)
    key_weight = scatter_about(key_of[2], (D, KV), D ** -0.5, 0.0625, ((0, 16), (1, 2)))
    key_grad = scatter_about(key_of[3], (TOKENS, KV), 1.0, 6.0, ((0, 384), (1, 2)))
    doc_lengths = jax.vmap(lambda own: uneven_parts(own, DOCS, TOK_DEV, TOK_DEV // 2, 1))(jax.random.split(key_of[4], MICRO)).reshape((MICRO, DOCS)).astype(jnp.int32)
    return {"activations": activations, "norm_gain": norm_gain, "key_weight": key_weight, "key_grad": key_grad, "doc_lengths": doc_lengths}


def positions(length_row, tok_rows):
    starts = jnp.cumsum(length_row) - length_row
    token_index = jnp.arange(tok_rows, dtype=jnp.int32)
    doc_first = lax.optimization_barrier(jnp.max(jnp.where(starts[None, :] <= token_index[:, None], starts[None, :], 0), axis=1))
    return (token_index - doc_first).astype(jnp.int32)

def normalize(act_block, norm_gain):
    widened = act_block.astype(jnp.float32)
    mean_square = lax.optimization_barrier(jnp.mean(widened * widened, axis=-1, keepdims=True))
    return (widened * lax.rsqrt(mean_square + 1e-06) * norm_gain.astype(jnp.float32)).astype(jnp.bfloat16)

def rope_back(grad_block, token_pos, head_count, head_size):
    half_size = head_size // 2
    frequency = jnp.exp(jnp.arange(half_size, dtype=jnp.float32) * (-2.0 * math.log(1000000.0) / head_size))
    angles = token_pos.astype(jnp.float32)[:, None] * frequency[None, :]
    cosine = jnp.cos(angles)[:, None, :]
    sine_part = jnp.sin(angles)[:, None, :]
    grad_heads = grad_block.astype(jnp.float32).reshape(grad_block.shape[0], head_count, head_size)
    first_half = grad_heads[..., :half_size]
    second_half = grad_heads[..., half_size:]
    rotated = jnp.concatenate([first_half * cosine + second_half * sine_part, second_half * cosine - first_half * sine_part], axis=-1)
    return rotated.reshape(grad_block.shape[0], head_count * head_size).astype(jnp.bfloat16)

def reference(activations, norm_gain, key_weight, key_grad, doc_lengths):
    micro_count = doc_lengths.shape[0]
    act_blocks = activations.reshape(micro_count, TOK_DEV, D)
    grad_blocks = key_grad.reshape(micro_count, TOK_DEV, KVH * HS)
    block_width = KVH * HS // N_TENSOR

    def scan_step(running, step_inputs):
        act_block, grad_block, len_block = step_inputs
        normed = normalize(act_block, norm_gain)
        rotated = rope_back(grad_block, positions(len_block, TOK_DEV), KVH, HS)
        grad_term = jnp.dot(normed.T, rotated, preferred_element_type=jnp.float32)
        summed = jnp.zeros((TOK_DEV, D), jnp.float32)
        for index in range(N_TENSOR):
            low = index * block_width
            product = jnp.dot(rotated[:, low:low + block_width], key_weight[:, low:low + block_width].T, preferred_element_type=jnp.float32)
            summed = summed + lax.optimization_barrier(product.astype(jnp.bfloat16)).astype(jnp.float32)
        return (running + grad_term, summed.astype(jnp.bfloat16))
    running, normed_rows = lax.scan(scan_step, jnp.zeros((D, KVH * HS), jnp.float32), (act_blocks, grad_blocks, doc_lengths))
    return (running / N_DP, normed_rows.reshape(micro_count * TOK_DEV, D))
```

```python
import functools
import math

import jax
import jax.numpy as jnp
from jax import lax
from jax.experimental import pallas as pl
from jax.experimental.pallas import tpu as pltpu
from jax.sharding import Mesh, PartitionSpec as P

NZ, NX, NY, NT = 12, 2, 8, 2
TOK, D, HS, COLS = 256, 8192, 128, 256
QUART = 128
FEAT = NY * QUART
KV = NT * COLS
ZROWS = 48
VMEM = 48 * 1024 * 1024
BF16, F32 = jnp.bfloat16, jnp.float32


def prep_kernel(place, doc, act, gain, key_grad, freq, *outs):
    xl, xh, t = place[0], place[1], place[2]
    rows = act.shape[0]
    square = jnp.zeros((rows, 128), F32)
    for j in range(D // 128):
        v = act[:, j * 128 : (j + 1) * 128].astype(F32)
        square = square + v * v
    scale = lax.rsqrt(jnp.sum(square, axis=1, keepdims=True) * (1.0 / D) + 1e-06)

    token = pl.program_id(0) * rows + lax.broadcasted_iota(jnp.int32, (rows, 128), 0)
    second = doc[0, 0]
    third = second + doc[0, 1]
    fourth = third + doc[0, 2]
    first = jnp.where(
        token >= fourth,
        fourth,
        jnp.where(token >= third, third, jnp.where(token >= second, second, 0)),
    )
    angle = (token - first).astype(F32) * freq[...]
    cosine = jnp.cos(angle)
    lane = lax.broadcasted_iota(jnp.int32, (rows, 128), 1)
    sine = jnp.sin(angle)
    sine = jnp.where(lane < HS // 2, sine, -sine)
    rotated = []
    for h in range(COLS // HS):
        v = key_grad[:, h * HS : (h + 1) * HS].astype(F32)
        rotated.append((v * cosine + pltpu.roll(v, HS // 2, 1) * sine).astype(BF16))

    for k, out in enumerate(outs):
        a, b = k & 1, k >> 1
        base = (xh ^ a) * (D // 2) + (2 * (xl ^ b) + t) * QUART
        for j in range(NY):
            at = pl.ds(pl.multiple_of(base + j * 4 * QUART, 128), QUART)
            v = act[:, at].astype(F32) * scale * gain[:, at]
            out[:, j * QUART : (j + 1) * QUART] = v.astype(BF16)
        for h, v in enumerate(rotated):
            out[:, FEAT + h * HS : FEAT + (h + 1) * HS] = v


def grad_kernel(place, b0, b1, b2, b3, other, out):
    t = place[2]
    blocks = (b0, b1, b2, b3)
    normed = jnp.concatenate([b[:, :FEAT] for b in blocks], axis=0)
    own = jnp.concatenate([b[:, FEAT:] for b in blocks], axis=0)
    for half, rot in ((t, own), (1 - t, other[...])):
        g = lax.dot_general(rot, normed, (((0,), (0,)), ((), ())), preferred_element_type=F32)
        g = g.astype(BF16)
        for y in range(NY):
            out[y, pl.ds(pl.multiple_of(half * COLS, COLS), COLS), :] = g[
                :, y * QUART : (y + 1) * QUART
            ]


def input_kernel(place, b0, b1, b2, b3, other, weight, *outs):
    t, swap = place[2], (place[1] ^ place[2]) == 1
    blocks = (b0, b1, b2, b3)
    lhs = []
    for r in range(4):
        own = jnp.where(swap, blocks[r ^ 1][:, FEAT:], blocks[r][:, FEAT:])
        oth = jnp.where(
            swap, other[(r ^ 1) * TOK : ((r ^ 1) + 1) * TOK, :], other[r * TOK : (r + 1) * TOK, :]
        )
        lhs.append(jnp.concatenate([own, oth], axis=1))
    lhs = jnp.concatenate(lhs, axis=0)
    for j in range(NY // 2):
        rhs = jnp.concatenate(
            [
                jnp.concatenate([weight[y, t], weight[y, 1 - t]], axis=1)
                for y in (2 * j, 2 * j + 1)
            ],
            axis=0,
        )
        p = lax.dot_general(lhs, rhs, (((1,), (1,)), ((), ())), preferred_element_type=F32)
        p = p.astype(BF16)
        for r, out in enumerate(outs):
            out[:, j * 2 * QUART : (j + 1) * 2 * QUART] = p[r * TOK : (r + 1) * TOK, :]


def place_kernel(place, r0, r1, r2, r3, out):
    mine = 2 * place[0] + place[1]
    for r, got in enumerate((r0, r1, r2, r3)):
        q = mine ^ r
        for y in range(NY):
            at = pl.ds(pl.multiple_of(y * 4 * QUART + q * QUART, QUART), QUART)
            out[:, at] = got[:, y * QUART : (y + 1) * QUART]


def whole(count):
    return [pl.BlockSpec(memory_space=pltpu.VMEM)] * count


SCALARS = pl.BlockSpec(memory_space=pltpu.SMEM)
PARAMS = pltpu.CompilerParams(vmem_limit_bytes=VMEM)


def per_device(activations, norm_gain, key_weight, key_grad, doc_lengths):
    xl, xh, t = lax.axis_index("xl"), lax.axis_index("xh"), lax.axis_index("t")
    place = jnp.stack([xl, xh, t]).astype(jnp.int32)
    half = jnp.arange(HS, dtype=jnp.int32) % (HS // 2)
    freq = jnp.exp(half.astype(F32) * (-2.0 * math.log(1000000.0) / HS))[None, :]

    rows = 64
    sent = jax.ShapeDtypeStruct((TOK, FEAT + COLS), BF16)
    blocks = pl.pallas_call(
        prep_kernel,
        grid=(TOK // rows,),
        in_specs=[
            SCALARS,
            SCALARS,
            pl.BlockSpec((rows, D), lambda i: (i, 0)),
            pl.BlockSpec((1, D), lambda i: (0, 0)),
            pl.BlockSpec((rows, COLS), lambda i: (i, 0)),
            pl.BlockSpec((1, HS), lambda i: (0, 0)),
        ],
        out_specs=[pl.BlockSpec((rows, FEAT + COLS), lambda i: (i, 0))] * 4,
        out_shape=[sent] * 4,
        compiler_params=PARAMS,
        name="prep",
    )(place, doc_lengths, activations, norm_gain[None, :], key_grad, freq)

    got = [blocks[0]] + [
        lax.ppermute(blocks[k], ("xl", "xh"), [(i, i ^ k) for i in range(4)]) for k in (1, 2, 3)
    ]

    shard = lax.dynamic_slice_in_dim(key_weight, xl * 2 * QUART, 2 * QUART, 0)
    shard = shard.reshape(1, NT, QUART, COLS)
    shard = jnp.broadcast_to(shard, (NY, NT, QUART, COLS)).reshape(NY * NT, QUART, COLS)
    weight = lax.all_to_all(shard, ("y", "t"), 0, 0, tiled=True).reshape(NY, NT, QUART, COLS)

    mine = jnp.concatenate([b[:, FEAT:] for b in got], axis=0)
    other = lax.ppermute(mine, "t", [(0, 1), (1, 0)])

    products = pl.pallas_call(
        input_kernel,
        in_specs=[SCALARS] + whole(6),
        out_specs=whole(4),
        out_shape=[jax.ShapeDtypeStruct((TOK, FEAT), BF16)] * 4,
        compiler_params=PARAMS,
        name="input_grad",
    )(place, *got, other, weight)

    returned = []
    for r in range(4):
        r0, r1 = r >> 1, r & 1
        pairs = [
            (4 * i + 2 * j + k, 4 * (i ^ r0) + 2 * (k ^ r1) + j)
            for i in range(2)
            for j in range(2)
            for k in range(2)
        ]
        returned.append(lax.ppermute(products[r], ("xl", "xh", "t"), pairs))

    term = pl.pallas_call(
        grad_kernel,
        in_specs=[SCALARS] + whole(5),
        out_specs=whole(1)[0],
        out_shape=jax.ShapeDtypeStruct((NY, KV, QUART), BF16),
        compiler_params=PARAMS,
        name="weight_grad",
    )(place, *got, other)

    term = lax.all_to_all(term, "y", 0, 0, tiled=True)
    term = jnp.sum(term.astype(F32), axis=0)
    term = jnp.pad(term, ((0, NZ * ZROWS - KV), (0, 0))).astype(BF16).reshape(NZ, ZROWS, QUART)
    term = lax.all_to_all(term, "z", 0, 0, tiled=True)
    term = jnp.sum(term.astype(F32), axis=0) * (1.0 / (NZ * NX))
    term = lax.all_gather(term, "z", axis=0, tiled=True)[:KV]
    term = jnp.broadcast_to(term.reshape(1, NT, COLS, QUART), (NX, NT, COLS, QUART))
    term = lax.all_to_all(term.reshape(NX * NT, COLS, QUART), ("xl", "t"), 0, 0, tiled=True)
    weight_grad = jnp.swapaxes(term, 1, 2).reshape(NX * NT * QUART, COLS)

    normed_grad = pl.pallas_call(
        place_kernel,
        grid=(TOK // rows,),
        in_specs=[SCALARS] + [pl.BlockSpec((rows, FEAT), lambda i: (i, 0))] * 4,
        out_specs=pl.BlockSpec((rows, 4 * FEAT), lambda i: (i, 0)),
        out_shape=jax.ShapeDtypeStruct((TOK, 4 * FEAT), BF16),
        compiler_params=PARAMS,
        name="placed",
    )(place, *returned)
    return (weight_grad, normed_grad)


def solution(mesh):
    fine = Mesh(mesh.devices.reshape(NZ, NX, 2, NY, NT), ("z", "xl", "xh", "y", "t"))
    tokens = ("z", "xl", "xh", "y")
    return jax.shard_map(
        per_device,
        mesh=fine,
        in_specs=(
            P(tokens, None),
            P(),
            P(("xh", "y"), "t"),
            P(tokens, "t"),
            P(tokens, None),
        ),
        out_specs=(P(("xh", "y"), "t"), P(tokens, "t")),
        check_vma=False,
    )
```

```python
import functools
import math

import jax
import jax.numpy as jnp
from jax import lax
from jax.experimental import pallas as pl
from jax.experimental.pallas import tpu as pltpu
from jax.sharding import Mesh, PartitionSpec as P

NZ, NX, NY, NT = 12, 2, 8, 2
TOK, D, HS, COLS = 256, 8192, 128, 256
QUART = 128
FEAT = NY * QUART
KV = NT * COLS
ZCOLS = 24
VMEM = 48 * 1024 * 1024
BF16, F32 = jnp.bfloat16, jnp.float32


def prep_kernel(place, act, gain, first, *outs):
    del first
    xl, xh, t = place[0], place[1], place[2]
    rows = act.shape[0]
    square = jnp.zeros((rows, 128), F32)
    for j in range(D // 128):
        v = act[:, j * 128 : (j + 1) * 128].astype(F32)
        square = square + v * v
    scale = lax.rsqrt(jnp.sum(square, axis=1, keepdims=True) * (1.0 / D) + 1e-06)

    for k, out in enumerate(outs):
        a, b = k & 1, k >> 1
        base = (xh ^ a) * (D // 2) + (2 * (xl ^ b) + t) * QUART
        for j in range(NY):
            at = pl.ds(pl.multiple_of(base + j * 4 * QUART, 128), QUART)
            v = act[:, at].astype(F32) * scale * gain[:, at]
            out[:, j * QUART : (j + 1) * QUART] = v.astype(BF16)


def rope_kernel(doc, key_grad, freq, first, rot):
    del first
    rows = key_grad.shape[0]
    token = lax.broadcasted_iota(jnp.int32, (rows, 128), 0)
    second = doc[0, 0]
    third = second + doc[0, 1]
    fourth = third + doc[0, 2]
    first = jnp.where(
        token >= fourth,
        fourth,
        jnp.where(token >= third, third, jnp.where(token >= second, second, 0)),
    )
    angle = (token - first).astype(F32) * freq[...]
    cosine = jnp.cos(angle)
    lane = lax.broadcasted_iota(jnp.int32, (rows, 128), 1)
    sine = jnp.sin(angle)
    sine = jnp.where(lane < HS // 2, sine, -sine)
    for h in range(COLS // HS):
        v = key_grad[:, h * HS : (h + 1) * HS].astype(F32)
        v = (v * cosine + pltpu.roll(v, HS // 2, 1) * sine).astype(BF16)
        for copy in range(4):
            rot[copy, :, h * HS : (h + 1) * HS] = v


def grad_kernel(place, b0, b1, b2, b3, mine, other, out):
    t, me = place[2], 2 * place[0] + place[1]
    normed = jnp.concatenate([b[...] for b in (b0, b1, b2, b3)], axis=0)
    for half, rot in ((t, mine), (1 - t, other)):
        rot = jnp.concatenate([rot[me ^ k] for k in range(4)], axis=0)
        g = lax.dot_general(rot, normed, (((0,), (0,)), ((), ())), preferred_element_type=F32)
        g = g.astype(BF16)
        for y in range(NY):
            out[y, pl.ds(pl.multiple_of(half * COLS, COLS), COLS), :] = g[
                :, y * QUART : (y + 1) * QUART
            ]


def input_kernel(place, mine, other, w_mine, w_other, *outs):
    xl, t = place[0], place[2]
    lhs = []
    for r in range(4):
        i = 2 * (xl ^ (r >> 1)) + (t ^ (r & 1))
        lhs.append(jnp.concatenate([mine[i], other[i]], axis=1))
    lhs = jnp.concatenate(lhs, axis=0)
    for j in range(NY // 2):
        rhs = jnp.concatenate(
            [
                jnp.concatenate([w_mine[y, t], w_other[y]], axis=1)
                for y in (2 * j, 2 * j + 1)
            ],
            axis=0,
        )
        p = lax.dot_general(lhs, rhs, (((1,), (1,)), ((), ())), preferred_element_type=F32)
        p = p.astype(BF16)
        for r, out in enumerate(outs):
            out[:, j * 2 * QUART : (j + 1) * 2 * QUART] = p[r * TOK : (r + 1) * TOK, :]


def sum_y_kernel(term, after, out):
    del after
    total = term[0].astype(F32)
    for y in range(1, NY):
        total = total + term[y].astype(F32)
    zero = jnp.zeros((NZ * ZCOLS - COLS, QUART), F32)
    for t in range(NT):
        padded = jnp.concatenate([total[t * COLS : (t + 1) * COLS, :], zero], axis=0)
        for z in range(NZ):
            out[z, t] = padded[z * ZCOLS : (z + 1) * ZCOLS, :].astype(BF16)


def sum_z_kernel(term, after0, after1, after2, after3, out):
    del after0, after1, after2, after3
    for t in range(NT):
        total = term[0, t].astype(F32)
        for z in range(1, NZ):
            total = total + term[z, t].astype(F32)
        total = (total * (1.0 / (NZ * NX))).astype(BF16)
        for z in range(NZ):
            out[z, t] = total


def split_kernel(term, out):
    for z in range(NZ):
        for t in range(NT):
            for xl in range(NX):
                out[NT * xl + t, z] = term[z, t]


def turn_kernel(term, out):
    for q in range(NX * NT):
        piece = jnp.concatenate([term[q, z].astype(F32) for z in range(NZ)], axis=0)
        out[q * QUART : (q + 1) * QUART, :] = piece[:COLS, :].T


def place_kernel(place, r0, r1, r2, r3, out):
    mine = 2 * place[0] + place[1]
    for r, got in enumerate((r0, r1, r2, r3)):
        q = mine ^ r
        for y in range(NY):
            at = pl.ds(pl.multiple_of(y * 4 * QUART + q * QUART, QUART), QUART)
            out[:, at] = got[:, y * QUART : (y + 1) * QUART]


def whole(count):
    return [pl.BlockSpec(memory_space=pltpu.VMEM)] * count


SCALARS = pl.BlockSpec(memory_space=pltpu.SMEM)
PARAMS = pltpu.CompilerParams(vmem_limit_bytes=VMEM)


def per_device(activations, norm_gain, key_weight, key_grad, doc_lengths):
    xl, xh, t = lax.axis_index("xl"), lax.axis_index("xh"), lax.axis_index("t")
    place = jnp.stack([xl, xh, t]).astype(jnp.int32)
    half = jnp.arange(HS, dtype=jnp.int32) % (HS // 2)
    freq = jnp.exp(half.astype(F32) * (-2.0 * math.log(1000000.0) / HS))[None, :]

    half_shard = lax.dynamic_slice_in_dim(key_weight, xl * NT * QUART, NT * QUART, 0)
    shard = lax.all_gather(half_shard, "y", axis=0, tiled=True).reshape(NY, NT, QUART, COLS)

    rotated = pl.pallas_call(
        rope_kernel,
        in_specs=[SCALARS] + whole(2) + [pl.BlockSpec(memory_space=pl.ANY)],
        out_specs=whole(1)[0],
        out_shape=jax.ShapeDtypeStruct((4, TOK, COLS), BF16),
        compiler_params=PARAMS,
        name="rope",
    )(doc_lengths, key_grad, freq, half_shard)
    rows = 64
    blocks = pl.pallas_call(
        prep_kernel,
        grid=(TOK // rows,),
        in_specs=[
            SCALARS,
            pl.BlockSpec((rows, D), lambda i: (i, 0)),
            pl.BlockSpec((1, D), lambda i: (0, 0)),
            pl.BlockSpec(memory_space=pl.ANY),
        ],
        out_specs=[pl.BlockSpec((rows, FEAT), lambda i: (i, 0))] * 4,
        out_shape=[jax.ShapeDtypeStruct((TOK, FEAT), BF16)] * 4,
        compiler_params=PARAMS,
        name="prep",
    )(place, activations, norm_gain[None, :], rotated)

    got = [blocks[0]] + [
        lax.ppermute(blocks[k], ("xl", "xh"), [(i, i ^ k) for i in range(4)]) for k in (1, 2, 3)
    ]
    mine = lax.all_to_all(rotated, ("xl", "xh"), 0, 0, tiled=True)
    other = lax.ppermute(mine, "t", [(0, 1), (1, 0)])

    term = pl.pallas_call(
        grad_kernel,
        in_specs=[SCALARS] + whole(6),
        out_specs=whole(1)[0],
        out_shape=jax.ShapeDtypeStruct((NY, KV, QUART), BF16),
        compiler_params=PARAMS,
        name="weight_grad",
    )(place, *got, mine, other)

    w_other = lax.dynamic_index_in_dim(shard, 1 - t, 1, keepdims=False)
    w_other = lax.ppermute(w_other, "t", [(0, 1), (1, 0)])
    products = pl.pallas_call(
        input_kernel,
        in_specs=[SCALARS] + whole(4),
        out_specs=whole(4),
        out_shape=[jax.ShapeDtypeStruct((TOK, FEAT), BF16)] * 4,
        compiler_params=PARAMS,
        name="input_grad",
    )(place, mine, other, shard, w_other)

    returned = []
    for r in range(4):
        r0, r1 = r >> 1, r & 1
        pairs = [
            (4 * i + 2 * j + k, 4 * (i ^ r0) + 2 * (k ^ r1) + j)
            for i in range(2)
            for j in range(2)
            for k in range(2)
        ]
        returned.append(lax.ppermute(products[r], ("xl", "xh", "t"), pairs))

    term = lax.all_to_all(term, "y", 0, 0, tiled=True)
    term = pl.pallas_call(
        sum_y_kernel,
        in_specs=whole(1) + [pl.BlockSpec(memory_space=pl.ANY)],
        out_specs=whole(1)[0],
        out_shape=jax.ShapeDtypeStruct((NZ, NT, ZCOLS, QUART), BF16),
        compiler_params=PARAMS,
        name="sum_y",
    )(term, products[0])
    term = lax.all_to_all(term, "z", 0, 0, tiled=True)
    pieces = jax.ShapeDtypeStruct((NZ, NT, ZCOLS, QUART), BF16)
    term = pl.pallas_call(
        sum_z_kernel,
        in_specs=whole(1) + [pl.BlockSpec(memory_space=pl.ANY)] * 4,
        out_specs=whole(1)[0],
        out_shape=pieces,
        compiler_params=PARAMS,
        name="sum_z",
    )(term, *returned)
    term = lax.all_to_all(term, "z", 0, 0, tiled=True)
    term = pl.pallas_call(
        split_kernel,
        in_specs=whole(1),
        out_specs=whole(1)[0],
        out_shape=jax.ShapeDtypeStruct((NX * NT, NZ, ZCOLS, QUART), BF16),
        compiler_params=PARAMS,
        name="split",
    )(term)
    term = lax.all_to_all(term, ("xl", "t"), 0, 0, tiled=True)
    weight_grad = pl.pallas_call(
        turn_kernel,
        in_specs=whole(1),
        out_specs=whole(1)[0],
        out_shape=jax.ShapeDtypeStruct((NX * NT * QUART, COLS), F32),
        compiler_params=PARAMS,
        name="turn",
    )(term)

    normed_grad = pl.pallas_call(
        place_kernel,
        grid=(TOK // rows,),
        in_specs=[SCALARS] + [pl.BlockSpec((rows, FEAT), lambda i: (i, 0))] * 4,
        out_specs=pl.BlockSpec((rows, 4 * FEAT), lambda i: (i, 0)),
        out_shape=jax.ShapeDtypeStruct((TOK, 4 * FEAT), BF16),
        compiler_params=PARAMS,
        name="placed",
    )(place, *returned)
    return (weight_grad, normed_grad)


def solution(mesh):
    fine = Mesh(mesh.devices.reshape(NZ, NX, 2, NY, NT), ("z", "xl", "xh", "y", "t"))
    tokens = ("z", "xl", "xh", "y")
    return jax.shard_map(
        per_device,
        mesh=fine,
        in_specs=(
            P(tokens, None),
            P(),
            P(("xh", "y"), "t"),
            P(tokens, "t"),
            P(tokens, None),
        ),
        out_specs=(P(("xh", "y"), "t"), P(tokens, "t")),
        check_vma=False,
    )
```

```python
import functools
import math

import jax
import jax.numpy as jnp
from jax import lax
from jax.experimental import pallas as pl
from jax.experimental.pallas import tpu as pltpu
from jax.sharding import Mesh, PartitionSpec as P

NZ, NX, NY, NT = 12, 2, 8, 2
TOK, D, HS, COLS = 256, 8192, 128, 256
QUART = 128
HALF = NY // 2
STEPS = (0, 4, 2, 6)
TOKEN = jax.ShapeDtypeStruct((8, 128), jnp.float32)
FEAT = NY * QUART
KV = NT * COLS
ZCOLS = 24
BF16, F32 = jnp.bfloat16, jnp.float32


def prep_kernel(doc, act, gain, key_grad, out, token_out):
    t = lax.axis_index("t")
    token_out[...] = jnp.zeros(TOKEN.shape, TOKEN.dtype)
    rows = act.shape[0]
    token = pl.program_id(0) * rows + lax.broadcasted_iota(jnp.int32, (rows, HS), 0)
    second = doc[0, 0]
    third = second + doc[0, 1]
    fourth = third + doc[0, 2]
    start = jnp.where(
        token >= fourth,
        fourth,
        jnp.where(token >= third, third, jnp.where(token >= second, second, 0)),
    )
    lane = lax.broadcasted_iota(jnp.int32, (rows, HS), 1)
    half = (lane[:1] % (HS // 2)).astype(F32)
    freq = jnp.exp(half * (-2.0 * math.log(1000000.0) / HS))
    angle = (token - start).astype(F32) * freq
    cosine = jnp.cos(angle)
    sine = jnp.sin(angle)
    sine = jnp.where(lane < HS // 2, sine, -sine)
    for h in range(COLS // HS):
        v = key_grad[:, h * HS : (h + 1) * HS].astype(F32)
        v = (v * cosine + pltpu.roll(v, HS // 2, 1) * sine).astype(BF16)
        for i in range(4):
            out[i, :, FEAT + h * HS : FEAT + (h + 1) * HS] = v

    square = jnp.zeros((rows, 128), F32)
    for j in range(D // 128):
        v = act[:, j * 128 : (j + 1) * 128].astype(F32)
        square = square + v * v
    scale = lax.rsqrt(jnp.sum(square, axis=1, keepdims=True) * (1.0 / D) + 1e-06)
    for i in range(4):
        base = (i & 1) * (D // 2) + (2 * (i >> 1) + t) * QUART
        for j in range(NY):
            at = pl.ds(pl.multiple_of(base + j * 4 * QUART, 128), QUART)
            v = act[:, at].astype(F32) * scale * gain[:, at]
            out[i, :, j * QUART : (j + 1) * QUART] = v.astype(BF16)


def half_kernel(weight, after, out):
    del after
    half = NT * QUART
    out[...] = weight[pl.ds(pl.multiple_of(lax.axis_index("xl") * half, half), half), :]


def pack_kernel(got, after, out):
    del after
    out[...] = got[...]


def product(rot, got):
    rot = rot.reshape(4 * TOK, COLS)
    normed = got[:, :, :FEAT].reshape(4 * TOK, FEAT)
    g = lax.dot_general(rot, normed, (((0,), (0,)), ((), ())), preferred_element_type=F32)
    return g.astype(BF16)


def own_kernel(got, out):
    g = product(got[:, :, FEAT:], got)
    for y in range(NY):
        out[y] = g[:, y * QUART : (y + 1) * QUART]


def grad_kernel(got, other, own, after, out):
    del after
    t = lax.axis_index("t")
    mine = pl.ds(pl.multiple_of(t * COLS, COLS), COLS)
    rest = pl.ds(pl.multiple_of((1 - t) * COLS, COLS), COLS)
    g = product(other[...], got)
    for y in range(NY):
        out[y, mine, :] = own[y]
        out[y, rest, :] = g[:, y * QUART : (y + 1) * QUART]


def other_kernel(near, far, out):
    rows = pl.ds(pl.multiple_of((1 - lax.axis_index("t")) * QUART, QUART), QUART)
    for k in range(HALF):
        out[k] = near[k, rows, :]
        out[HALF + k] = far[k, rows, :]


def input_kernel(mine, other, near, far, w_other, *outs):
    outs, token = outs[:4], outs[4]
    token[...] = jnp.zeros(TOKEN.shape, TOKEN.dtype)
    xl, t, y = lax.axis_index("xl"), lax.axis_index("t"), lax.axis_index("y")
    lhs = []
    for r in range(4):
        i = 2 * (xl ^ (r >> 1)) + (t ^ (r & 1))
        lhs.append(jnp.concatenate([mine[i], other[i]], axis=1))
    lhs = jnp.concatenate(lhs, axis=0)
    own = pl.ds(pl.multiple_of(t * QUART, QUART), QUART)
    for half, weight in enumerate((near, far)):
        for j in range(0, HALF, 2):
            rhs = jnp.concatenate(
                [
                    jnp.concatenate([weight[k, own, :], w_other[HALF * half + k]], axis=1)
                    for k in (j, j + 1)
                ],
                axis=0,
            )
            p = lax.dot_general(lhs, rhs, (((1,), (1,)), ((), ())), preferred_element_type=F32)
            p = p.astype(BF16)
            for k in (j, j + 1):
                at = pl.ds(pl.multiple_of((y ^ STEPS[k] ^ half) * QUART, QUART), QUART)
                for r, out in enumerate(outs):
                    out[:, at] = p[r * TOK : (r + 1) * TOK, (k - j) * QUART : (k - j + 1) * QUART]


def sum_y_kernel(term, after, out):
    del after
    total = term[0].astype(F32)
    for y in range(1, NY):
        total = total + term[y].astype(F32)
    zero = jnp.zeros((NZ * ZCOLS - COLS, QUART), F32)
    for t in range(NT):
        padded = jnp.concatenate([total[t * COLS : (t + 1) * COLS, :], zero], axis=0)
        for z in range(NZ):
            out[z, t] = padded[z * ZCOLS : (z + 1) * ZCOLS, :].astype(BF16)


def sum_z_kernel(term, after0, after1, after2, after3, out):
    del after0, after1, after2, after3
    for t in range(NT):
        total = term[0, t].astype(F32)
        for z in range(1, NZ):
            total = total + term[z, t].astype(F32)
        total = (total * (1.0 / (NZ * NX))).astype(BF16)
        for z in range(NZ):
            out[z, t] = total


def split_kernel(term, after, out):
    del after
    for z in range(NZ):
        for t in range(NT):
            for xl in range(NX):
                out[NT * xl + t, z] = term[z, t]


def turn_kernel(term, out):
    for q in range(NX * NT):
        piece = jnp.concatenate([term[q, z].astype(F32) for z in range(NZ)], axis=0)
        out[q * QUART : (q + 1) * QUART, :] = piece[:COLS, :].T


def place_kernel(r0, r1, r2, r3, out, token):
    token[...] = jnp.zeros(TOKEN.shape, TOKEN.dtype)
    mine = 2 * lax.axis_index("xl") + lax.axis_index("xh")
    for r, got in enumerate((r0, r1, r2, r3)):
        q = mine ^ r
        for y in range(NY):
            at = pl.ds(pl.multiple_of(y * 4 * QUART + q * QUART, QUART), QUART)
            out[:, at] = got[:, y * QUART : (y + 1) * QUART]


def whole(count):
    return [pl.BlockSpec(memory_space=pltpu.VMEM)] * count


UNUSED = [pl.BlockSpec(memory_space=pl.ANY)]
SCALARS = pl.BlockSpec(memory_space=pltpu.SMEM)
PARAMS = pltpu.CompilerParams(vmem_limit_bytes=48 * 1024 * 1024)
LARGE = pltpu.CompilerParams(vmem_limit_bytes=60 * 1024 * 1024)


def per_device(activations, norm_gain, key_weight, key_grad, doc_lengths):
    rows = 64
    blocks, prepared = pl.pallas_call(
        prep_kernel,
        grid=(TOK // rows,),
        in_specs=[
            SCALARS,
            pl.BlockSpec((rows, D), lambda i: (i, 0)),
            pl.BlockSpec((1, D), lambda i: (0, 0)),
            pl.BlockSpec((rows, COLS), lambda i: (i, 0)),
        ],
        out_specs=[
            pl.BlockSpec((4, rows, FEAT + COLS), lambda i: (0, i, 0)),
            pl.BlockSpec(TOKEN.shape, lambda i: (0, 0)),
        ],
        out_shape=[jax.ShapeDtypeStruct((4, TOK, FEAT + COLS), BF16), TOKEN],
        compiler_params=LARGE,
        name="prep",
    )(doc_lengths, activations, norm_gain[None, :], key_grad)

    got = lax.all_to_all(blocks, ("xl", "xh"), 0, 0, tiled=True)

    half_weight = pl.pallas_call(
        half_kernel,
        in_specs=whole(1) + UNUSED,
        out_specs=whole(1)[0],
        out_shape=jax.ShapeDtypeStruct((NT * QUART, COLS), BF16),
        compiler_params=PARAMS,
        name="half_weight",
    )(key_weight, prepared)
    near = jnp.stack(
        [half_weight]
        + [lax.ppermute(half_weight, "y", [(i, i ^ e) for i in range(NY)]) for e in STEPS[1:]]
    )
    far = lax.ppermute(near, "y", [(i, i ^ 1) for i in range(NY)])

    mine = pl.pallas_call(
        pack_kernel,
        grid=(1,),
        in_specs=[pl.BlockSpec((4, TOK, COLS), lambda i: (0, 0, FEAT // COLS))] + UNUSED,
        out_specs=pl.BlockSpec((4, TOK, COLS), lambda i: (0, 0, 0)),
        out_shape=jax.ShapeDtypeStruct((4, TOK, COLS), BF16),
        compiler_params=PARAMS,
        name="pack",
    )(got, near)
    other = lax.ppermute(mine, "t", [(0, 1), (1, 0)])

    term = pl.pallas_call(
        own_kernel,
        in_specs=whole(1),
        out_specs=whole(1)[0],
        out_shape=jax.ShapeDtypeStruct((NY, COLS, QUART), BF16),
        compiler_params=PARAMS,
        name="own_grad",
    )(got)
    term = pl.pallas_call(
        grad_kernel,
        in_specs=whole(3) + UNUSED,
        out_specs=whole(1)[0],
        out_shape=jax.ShapeDtypeStruct((NY, KV, QUART), BF16),
        compiler_params=PARAMS,
        name="weight_grad",
    )(got, other, term, far)

    w_other = pl.pallas_call(
        other_kernel,
        in_specs=whole(2),
        out_specs=whole(1)[0],
        out_shape=jax.ShapeDtypeStruct((NY, QUART, COLS), BF16),
        compiler_params=PARAMS,
        name="w_other",
    )(near, far)
    w_other = lax.ppermute(w_other, "t", [(0, 1), (1, 0)])
    *products, multiplied = pl.pallas_call(
        input_kernel,
        in_specs=whole(5),
        out_specs=whole(5),
        out_shape=[jax.ShapeDtypeStruct((TOK, FEAT), BF16)] * 4 + [TOKEN],
        compiler_params=PARAMS,
        name="input_grad",
    )(mine, other, near, far, w_other)

    returned = []
    for r in range(4):
        r0, r1 = r >> 1, r & 1
        pairs = [
            (4 * i + 2 * j + k, 4 * (i ^ r0) + 2 * (k ^ r1) + j)
            for i in range(2)
            for j in range(2)
            for k in range(2)
        ]
        returned.append(lax.ppermute(products[r], ("xl", "xh", "t"), pairs))

    term = lax.all_to_all(term, "y", 0, 0, tiled=True)
    term = pl.pallas_call(
        sum_y_kernel,
        in_specs=whole(1) + [pl.BlockSpec(memory_space=pl.ANY)],
        out_specs=whole(1)[0],
        out_shape=jax.ShapeDtypeStruct((NZ, NT, ZCOLS, QUART), BF16),
        compiler_params=PARAMS,
        name="sum_y",
    )(term, multiplied)
    term = lax.all_to_all(term, "z", 0, 0, tiled=True)
    normed_grad, placed = pl.pallas_call(
        place_kernel,
        grid=(TOK // rows,),
        in_specs=[pl.BlockSpec((rows, FEAT), lambda i: (i, 0))] * 4,
        out_specs=[
            pl.BlockSpec((rows, 4 * FEAT), lambda i: (i, 0)),
            pl.BlockSpec(TOKEN.shape, lambda i: (0, 0)),
        ],
        out_shape=[jax.ShapeDtypeStruct((TOK, 4 * FEAT), BF16), TOKEN],
        compiler_params=PARAMS,
        name="placed",
    )(*returned)
    pieces = jax.ShapeDtypeStruct((NZ, NT, ZCOLS, QUART), BF16)
    term = pl.pallas_call(
        sum_z_kernel,
        in_specs=whole(1) + [pl.BlockSpec(memory_space=pl.ANY)] * 4,
        out_specs=whole(1)[0],
        out_shape=pieces,
        compiler_params=PARAMS,
        name="sum_z",
    )(term, *returned)
    term = lax.all_to_all(term, "z", 0, 0, tiled=True)
    term = pl.pallas_call(
        split_kernel,
        in_specs=whole(1) + UNUSED,
        out_specs=whole(1)[0],
        out_shape=jax.ShapeDtypeStruct((NX * NT, NZ, ZCOLS, QUART), BF16),
        compiler_params=PARAMS,
        name="split",
    )(term, placed)
    term = lax.all_to_all(term, ("xl", "t"), 0, 0, tiled=True)
    weight_grad = pl.pallas_call(
        turn_kernel,
        in_specs=whole(1),
        out_specs=whole(1)[0],
        out_shape=jax.ShapeDtypeStruct((NX * NT * QUART, COLS), F32),
        compiler_params=PARAMS,
        name="turn",
    )(term)

    return (weight_grad, normed_grad)


def solution(mesh):
    fine = Mesh(mesh.devices.reshape(NZ, NX, 2, NY, NT), ("z", "xl", "xh", "y", "t"))
    tokens = ("z", "xl", "xh", "y")
    return jax.shard_map(
        per_device,
        mesh=fine,
        in_specs=(
            P(tokens, None),
            P(),
            P(("xh", "y"), "t"),
            P(tokens, "t"),
            P(tokens, None),
        ),
        out_specs=(P(("xh", "y"), "t"), P(tokens, "t")),
        check_vma=False,
    )
```

```python
import functools
import math

import jax
import jax.numpy as jnp
from jax import lax
from jax.experimental import pallas as pl
from jax.experimental.pallas import tpu as pltpu
from jax.sharding import Mesh, PartitionSpec as P

NZ, NX, NY, NT = 12, 2, 8, 2
TOK, D, HS, COLS = 256, 8192, 128, 256
QUART = 128
HALF = NY // 2
STEPS = (0, 6, 2, 4)
TOKEN = jax.ShapeDtypeStruct((8, 128), jnp.float32)
FEAT = NY * QUART
KV = NT * COLS
ZCOLS = 24
BF16, F32 = jnp.bfloat16, jnp.float32


def prep_kernel(doc, act, gain, key_grad, out, token_out):
    t = lax.axis_index("t")
    token_out[...] = jnp.zeros(TOKEN.shape, TOKEN.dtype)
    rows = act.shape[0]
    token = pl.program_id(0) * rows + lax.broadcasted_iota(jnp.int32, (rows, HS), 0)
    second = doc[0, 0]
    third = second + doc[0, 1]
    fourth = third + doc[0, 2]
    start = jnp.where(
        token >= fourth,
        fourth,
        jnp.where(token >= third, third, jnp.where(token >= second, second, 0)),
    )
    lane = lax.broadcasted_iota(jnp.int32, (rows, HS), 1)
    half = (lane[:1] % (HS // 2)).astype(F32)
    freq = jnp.exp(half * (-2.0 * math.log(1000000.0) / HS))
    angle = (token - start).astype(F32) * freq
    cosine = jnp.cos(angle)
    sine = jnp.sin(angle)
    sine = jnp.where(lane < HS // 2, sine, -sine)
    for h in range(COLS // HS):
        v = key_grad[:, h * HS : (h + 1) * HS].astype(F32)
        v = (v * cosine + pltpu.roll(v, HS // 2, 1) * sine).astype(BF16)
        for i in range(4):
            out[i, :, FEAT + h * HS : FEAT + (h + 1) * HS] = v

    square = jnp.zeros((rows, 128), F32)
    for j in range(D // 128):
        v = act[:, j * 128 : (j + 1) * 128].astype(F32)
        square = square + v * v
    scale = lax.rsqrt(jnp.sum(square, axis=1, keepdims=True) * (1.0 / D) + 1e-06)
    for i in range(4):
        base = (i & 1) * (D // 2) + (2 * (i >> 1) + t) * QUART
        for j in range(NY):
            at = pl.ds(pl.multiple_of(base + j * 4 * QUART, 128), QUART)
            v = act[:, at].astype(F32) * scale * gain[:, at]
            out[i, :, j * QUART : (j + 1) * QUART] = v.astype(BF16)


def half_kernel(weight, after, out):
    del after
    half = NT * QUART
    out[...] = weight[pl.ds(pl.multiple_of(lax.axis_index("xl") * half, half), half), :]


def pack_kernel(got, after, out):
    del after
    out[...] = got[...]


def product(rot, got):
    rot = rot.reshape(4 * TOK, COLS)
    normed = got[:, :, :FEAT].reshape(4 * TOK, FEAT)
    g = lax.dot_general(rot, normed, (((0,), (0,)), ((), ())), preferred_element_type=F32)
    return g.astype(BF16)


def own_kernel(got, out):
    g = product(got[:, :, FEAT:], got)
    for y in range(NY):
        out[y] = g[:, y * QUART : (y + 1) * QUART]


def grad_kernel(got, other, own, after, out):
    del after
    t = lax.axis_index("t")
    mine = pl.ds(pl.multiple_of(t * COLS, COLS), COLS)
    rest = pl.ds(pl.multiple_of((1 - t) * COLS, COLS), COLS)
    g = product(other[...], got)
    for y in range(NY):
        out[y, mine, :] = own[y]
        out[y, rest, :] = g[:, y * QUART : (y + 1) * QUART]


def other_kernel(mine, near, far, out):
    out[: 4 * TOK, :] = mine[...].reshape(4 * TOK, COLS)
    rows = pl.ds(pl.multiple_of((1 - lax.axis_index("t")) * QUART, QUART), QUART)
    for k in range(NY):
        shard = near[k, rows, :] if k < HALF else far[k - HALF, rows, :]
        out[4 * TOK + k * QUART : 4 * TOK + (k + 1) * QUART, :] = shard


def input_kernel(mine, near, far, other, *outs):
    outs, token = outs[:4], outs[4]
    token[...] = jnp.zeros(TOKEN.shape, TOKEN.dtype)
    xl, t = lax.axis_index("xl"), lax.axis_index("t")
    own = pl.ds(pl.multiple_of(t * QUART, QUART), QUART)

    def multiply(weight, h):
        lhs = []
        for r in range(4):
            i = 2 * (xl ^ (r >> 1)) + (t ^ (r & 1))
            rows = pl.ds(pl.multiple_of(i * TOK, TOK), TOK)
            lhs.append(jnp.concatenate([mine[i], other[rows, :]], axis=1))
        lhs = jnp.concatenate(lhs, axis=0)
        for j in range(0, HALF, 2):
            at = 4 * TOK + (HALF * h + j) * QUART
            rhs = jnp.concatenate(
                [
                    jnp.concatenate([weight[j + k, own, :] for k in range(2)], axis=0),
                    other[at : at + 2 * QUART, :],
                ],
                axis=1,
            )
            p = lax.dot_general(lhs, rhs, (((1,), (1,)), ((), ())), preferred_element_type=F32)
            p = p.astype(BF16)
            for r, out in enumerate(outs):
                out[:, j * QUART : (j + 2) * QUART] = p[r * TOK : (r + 1) * TOK, :]

    pl.when(pl.program_id(0) == 0)(functools.partial(multiply, near, 0))
    pl.when(pl.program_id(0) == 1)(functools.partial(multiply, far, 1))


def sum_y_kernel(term, after, out):
    del after
    total = term[0].astype(F32)
    for y in range(1, NY):
        total = total + term[y].astype(F32)
    zero = jnp.zeros((NZ * ZCOLS - COLS, QUART), F32)
    for t in range(NT):
        padded = jnp.concatenate([total[t * COLS : (t + 1) * COLS, :], zero], axis=0)
        for z in range(NZ):
            out[z, t] = padded[z * ZCOLS : (z + 1) * ZCOLS, :].astype(BF16)


def sum_z_kernel(term, after0, after1, after2, after3, out):
    del after0, after1, after2, after3
    for t in range(NT):
        total = term[0, t].astype(F32)
        for z in range(1, NZ):
            total = total + term[z, t].astype(F32)
        total = (total * (1.0 / (NZ * NX))).astype(BF16)
        for z in range(NZ):
            out[z, t] = total


def split_kernel(term, after, out):
    del after
    for z in range(NZ):
        for t in range(NT):
            for xl in range(NX):
                out[NT * xl + t, z] = term[z, t]


def turn_kernel(term, out):
    for q in range(NX * NT):
        piece = jnp.concatenate([term[q, z].astype(F32) for z in range(NZ)], axis=0)
        out[q * QUART : (q + 1) * QUART, :] = piece[:COLS, :].T


def place_kernel(r0, r1, r2, r3, out, token):
    token[...] = jnp.zeros(TOKEN.shape, TOKEN.dtype)
    mine, y = 2 * lax.axis_index("xl") + lax.axis_index("xh"), lax.axis_index("y")
    for r, got in enumerate((r0, r1, r2, r3)):
        q = mine ^ r
        for k in range(NY):
            block = y ^ STEPS[k % HALF] ^ (k // HALF)
            at = pl.ds(pl.multiple_of(block * 4 * QUART + q * QUART, QUART), QUART)
            out[:, at] = got[:, k * QUART : (k + 1) * QUART]


def whole(count):
    return [pl.BlockSpec(memory_space=pltpu.VMEM)] * count


UNUSED = [pl.BlockSpec(memory_space=pl.ANY)]
SCALARS = pl.BlockSpec(memory_space=pltpu.SMEM)
PARAMS = pltpu.CompilerParams(vmem_limit_bytes=48 * 1024 * 1024)
LARGE = pltpu.CompilerParams(vmem_limit_bytes=60 * 1024 * 1024)


def per_device(activations, norm_gain, key_weight, key_grad, doc_lengths):
    rows = 128
    blocks, prepared = pl.pallas_call(
        prep_kernel,
        grid=(TOK // rows,),
        in_specs=[
            SCALARS,
            pl.BlockSpec((rows, D), lambda i: (i, 0)),
            pl.BlockSpec((1, D), lambda i: (0, 0)),
            pl.BlockSpec((rows, COLS), lambda i: (i, 0)),
        ],
        out_specs=[
            pl.BlockSpec((4, rows, FEAT + COLS), lambda i: (0, i, 0)),
            pl.BlockSpec(TOKEN.shape, lambda i: (0, 0)),
        ],
        out_shape=[jax.ShapeDtypeStruct((4, TOK, FEAT + COLS), BF16), TOKEN],
        compiler_params=LARGE,
        name="prep",
    )(doc_lengths, activations, norm_gain[None, :], key_grad)

    got = lax.all_to_all(blocks, ("xl", "xh"), 0, 0, tiled=True)

    half_weight = pl.pallas_call(
        half_kernel,
        in_specs=whole(1) + UNUSED,
        out_specs=whole(1)[0],
        out_shape=jax.ShapeDtypeStruct((NT * QUART, COLS), BF16),
        compiler_params=PARAMS,
        name="half_weight",
    )(key_weight, prepared)
    near = jnp.stack(
        [half_weight]
        + [lax.ppermute(half_weight, "y", [(i, i ^ e) for i in range(NY)]) for e in STEPS[1:]]
    )
    far = lax.ppermute(near, "y", [(i, i ^ 1) for i in range(NY)])

    mine = pl.pallas_call(
        pack_kernel,
        grid=(1,),
        in_specs=[pl.BlockSpec((4, TOK, COLS), lambda i: (0, 0, FEAT // COLS))] + UNUSED,
        out_specs=pl.BlockSpec((4, TOK, COLS), lambda i: (0, 0, 0)),
        out_shape=jax.ShapeDtypeStruct((4, TOK, COLS), BF16),
        compiler_params=PARAMS,
        name="pack",
    )(got, near)
    other = lax.ppermute(mine, "t", [(0, 1), (1, 0)])

    term = pl.pallas_call(
        own_kernel,
        in_specs=whole(1),
        out_specs=whole(1)[0],
        out_shape=jax.ShapeDtypeStruct((NY, COLS, QUART), BF16),
        compiler_params=PARAMS,
        name="own_grad",
    )(got)
    term = pl.pallas_call(
        grad_kernel,
        in_specs=whole(3) + UNUSED,
        out_specs=whole(1)[0],
        out_shape=jax.ShapeDtypeStruct((NY, KV, QUART), BF16),
        compiler_params=PARAMS,
        name="weight_grad",
    )(got, other, term, far)

    swapped = pl.pallas_call(
        other_kernel,
        in_specs=whole(3),
        out_specs=whole(1)[0],
        out_shape=jax.ShapeDtypeStruct((4 * TOK + FEAT, COLS), BF16),
        compiler_params=PARAMS,
        name="to_other",
    )(mine, near, far)
    swapped = lax.ppermute(swapped, "t", [(0, 1), (1, 0)])
    shards = pl.BlockSpec((4, TOK, COLS), lambda i: (0, 0, 0))
    *products, multiplied = pl.pallas_call(
        input_kernel,
        grid=(2,),
        in_specs=[shards] * 3 + [pl.BlockSpec((4 * TOK + FEAT, COLS), lambda i: (0, 0))],
        out_specs=[pl.BlockSpec((TOK, FEAT // 2), lambda i: (0, i))] * 4
        + [pl.BlockSpec(TOKEN.shape, lambda i: (0, 0))],
        out_shape=[jax.ShapeDtypeStruct((TOK, FEAT), BF16)] * 4 + [TOKEN],
        compiler_params=PARAMS,
        name="input_grad",
    )(mine, near, far, swapped)

    returned = []
    for r in range(4):
        r0, r1 = r >> 1, r & 1
        pairs = [
            (4 * i + 2 * j + k, 4 * (i ^ r0) + 2 * (k ^ r1) + j)
            for i in range(2)
            for j in range(2)
            for k in range(2)
        ]
        returned.append(lax.ppermute(products[r], ("xl", "xh", "t"), pairs))

    term = lax.all_to_all(term, "y", 0, 0, tiled=True)
    term = pl.pallas_call(
        sum_y_kernel,
        in_specs=whole(1) + [pl.BlockSpec(memory_space=pl.ANY)],
        out_specs=whole(1)[0],
        out_shape=jax.ShapeDtypeStruct((NZ, NT, ZCOLS, QUART), BF16),
        compiler_params=PARAMS,
        name="sum_y",
    )(term, multiplied)
    term = lax.all_to_all(term, "z", 0, 0, tiled=True)
    rows = 64
    normed_grad, placed = pl.pallas_call(
        place_kernel,
        grid=(TOK // rows,),
        in_specs=[pl.BlockSpec((rows, FEAT), lambda i: (i, 0))] * 4,
        out_specs=[
            pl.BlockSpec((rows, 4 * FEAT), lambda i: (i, 0)),
            pl.BlockSpec(TOKEN.shape, lambda i: (0, 0)),
        ],
        out_shape=[jax.ShapeDtypeStruct((TOK, 4 * FEAT), BF16), TOKEN],
        compiler_params=PARAMS,
        name="placed",
    )(*returned)
    pieces = jax.ShapeDtypeStruct((NZ, NT, ZCOLS, QUART), BF16)
    term = pl.pallas_call(
        sum_z_kernel,
        in_specs=whole(1) + [pl.BlockSpec(memory_space=pl.ANY)] * 4,
        out_specs=whole(1)[0],
        out_shape=pieces,
        compiler_params=PARAMS,
        name="sum_z",
    )(term, *returned)
    term = lax.all_to_all(term, "z", 0, 0, tiled=True)
    term = pl.pallas_call(
        split_kernel,
        in_specs=whole(1) + UNUSED,
        out_specs=whole(1)[0],
        out_shape=jax.ShapeDtypeStruct((NX * NT, NZ, ZCOLS, QUART), BF16),
        compiler_params=PARAMS,
        name="split",
    )(term, placed)
    term = lax.all_to_all(term, ("xl", "t"), 0, 0, tiled=True)
    weight_grad = pl.pallas_call(
        turn_kernel,
        in_specs=whole(1),
        out_specs=whole(1)[0],
        out_shape=jax.ShapeDtypeStruct((NX * NT * QUART, COLS), F32),
        compiler_params=PARAMS,
        name="turn",
    )(term)

    return (weight_grad, normed_grad)


def solution(mesh):
    fine = Mesh(mesh.devices.reshape(NZ, NX, 2, NY, NT), ("z", "xl", "xh", "y", "t"))
    tokens = ("z", "xl", "xh", "y")
    return jax.shard_map(
        per_device,
        mesh=fine,
        in_specs=(
            P(tokens, None),
            P(),
            P(("xh", "y"), "t"),
            P(tokens, "t"),
            P(tokens, None),
        ),
        out_specs=(P(("xh", "y"), "t"), P(tokens, "t")),
        check_vma=False,
    )
```

```python
import functools
import math

import jax
import jax.numpy as jnp
from jax import lax
from jax.experimental import pallas as pl
from jax.experimental.pallas import tpu as pltpu
from jax.sharding import Mesh, PartitionSpec as P

NZ, NX, NY, NT = 12, 2, 8, 2
TOK, D, HS, COLS = 256, 8192, 128, 256
QUART = 128
HALF = NY // 2
STEPS = (0, 6, 2, 4)
TOKEN = jax.ShapeDtypeStruct((8, 128), jnp.float32)
FEAT = NY * QUART
KV = NT * COLS
LAST_FIRST = [list(range(NY - 1, -1, -1))]
ALONG_Z = [[(7 - p) % NZ for p in range(NZ)]]
ZCOLS = 24
BF16, F32 = jnp.bfloat16, jnp.float32


def prep_kernel(doc, act, gain, key_grad, out, token_out):
    t = lax.axis_index("t")
    token_out[...] = jnp.zeros(TOKEN.shape, TOKEN.dtype)
    rows = act.shape[0]
    token = pl.program_id(0) * rows + lax.broadcasted_iota(jnp.int32, (rows, HS), 0)
    second = doc[0, 0]
    third = second + doc[0, 1]
    fourth = third + doc[0, 2]
    start = jnp.where(
        token >= fourth,
        fourth,
        jnp.where(token >= third, third, jnp.where(token >= second, second, 0)),
    )
    lane = lax.broadcasted_iota(jnp.int32, (rows, HS), 1)
    half = (lane[:1] % (HS // 2)).astype(F32)
    freq = jnp.exp(half * (-2.0 * math.log(1000000.0) / HS))
    angle = (token - start).astype(F32) * freq
    cosine = jnp.cos(angle)
    sine = jnp.sin(angle)
    sine = jnp.where(lane < HS // 2, sine, -sine)
    for h in range(COLS // HS):
        v = key_grad[:, h * HS : (h + 1) * HS].astype(F32)
        v = (v * cosine + pltpu.roll(v, HS // 2, 1) * sine).astype(BF16)
        for i in range(4):
            out[i, :, FEAT + h * HS : FEAT + (h + 1) * HS] = v

    square = jnp.zeros((rows, 128), F32)
    for j in range(D // 128):
        v = act[:, j * 128 : (j + 1) * 128].astype(F32)
        square = square + v * v
    scale = lax.rsqrt(jnp.sum(square, axis=1, keepdims=True) * (1.0 / D) + 1e-06)
    for i in range(4):
        base = (i & 1) * (D // 2) + (2 * (i >> 1) + t) * QUART
        for j in range(NY):
            at = pl.ds(pl.multiple_of(base + j * 4 * QUART, 128), QUART)
            v = act[:, at].astype(F32) * scale * gain[:, at]
            out[i, :, j * QUART : (j + 1) * QUART] = v.astype(BF16)


def half_kernel(weight, after, out):
    del after
    half = NT * QUART
    out[...] = weight[pl.ds(pl.multiple_of(lax.axis_index("xl") * half, half), half), :]


def pack_kernel(got, after, out):
    del after
    out[...] = got[...]


def product(rot, got):
    rot = rot.reshape(4 * TOK, COLS)
    normed = got[:, :, :FEAT].reshape(4 * TOK, FEAT)
    g = lax.dot_general(rot, normed, (((0,), (0,)), ((), ())), preferred_element_type=F32)
    return g.astype(BF16)


def own_kernel(got, out):
    g = product(got[:, :, FEAT:], got)
    for y in range(NY):
        out[y] = g[:, y * QUART : (y + 1) * QUART]


def grad_kernel(got, other, own, after, out):
    del after
    t = lax.axis_index("t")
    mine = pl.ds(pl.multiple_of(t * COLS, COLS), COLS)
    rest = pl.ds(pl.multiple_of((1 - t) * COLS, COLS), COLS)
    g = product(other[...], got)
    for y in range(NY):
        place = NY - 1 - y
        out[place, mine, :] = own[y]
        out[place, rest, :] = g[:, y * QUART : (y + 1) * QUART]


def other_kernel(mine, near, far, out):
    out[: 4 * TOK, :] = mine[...].reshape(4 * TOK, COLS)
    rows = pl.ds(pl.multiple_of((1 - lax.axis_index("t")) * QUART, QUART), QUART)
    for k in range(NY):
        shard = near[k, rows, :] if k < HALF else far[k - HALF, rows, :]
        out[4 * TOK + k * QUART : 4 * TOK + (k + 1) * QUART, :] = shard


def input_kernel(mine, near, far, other, *outs):
    outs, token = outs[:4], outs[4]
    token[...] = jnp.zeros(TOKEN.shape, TOKEN.dtype)
    xl, t = lax.axis_index("xl"), lax.axis_index("t")
    own = pl.ds(pl.multiple_of(t * QUART, QUART), QUART)

    def multiply(weight, h):
        lhs = []
        for r in range(4):
            i = 2 * (xl ^ (r >> 1)) + (t ^ (r & 1))
            rows = pl.ds(pl.multiple_of(i * TOK, TOK), TOK)
            lhs.append(jnp.concatenate([mine[i], other[rows, :]], axis=1))
        lhs = jnp.concatenate(lhs, axis=0)
        for j in range(0, HALF, 2):
            at = 4 * TOK + (HALF * h + j) * QUART
            rhs = jnp.concatenate(
                [
                    jnp.concatenate([weight[j + k, own, :] for k in range(2)], axis=0),
                    other[at : at + 2 * QUART, :],
                ],
                axis=1,
            )
            p = lax.dot_general(lhs, rhs, (((1,), (1,)), ((), ())), preferred_element_type=F32)
            p = p.astype(BF16)
            for r, out in enumerate(outs):
                out[:, j * QUART : (j + 2) * QUART] = p[r * TOK : (r + 1) * TOK, :]

    pl.when(pl.program_id(0) == 0)(functools.partial(multiply, near, 0))
    pl.when(pl.program_id(0) == 1)(functools.partial(multiply, far, 1))


def sum_y_kernel(term, after, out):
    del after
    total = term[0].astype(F32)
    for y in range(1, NY):
        total = total + term[y].astype(F32)
    zero = jnp.zeros((NZ * ZCOLS - COLS, QUART), F32)
    for t in range(NT):
        padded = jnp.concatenate([total[t * COLS : (t + 1) * COLS, :], zero], axis=0)
        for z in range(NZ):
            out[z, t] = padded[z * ZCOLS : (z + 1) * ZCOLS, :].astype(BF16)


def sum_z_kernel(term, after0, after1, after2, after3, out):
    del after0, after1, after2, after3
    for t in range(NT):
        total = term[0, t].astype(F32)
        for z in range(1, NZ):
            total = total + term[z, t].astype(F32)
        total = (total * (1.0 / (NZ * NX))).astype(BF16)
        for z in range(NZ):
            out[z, t] = total


def split_kernel(term, after, out):
    del after
    for z in range(NZ):
        for t in range(NT):
            for xl in range(NX):
                out[NT * xl + t, z] = term[z, t]


def turn_kernel(term, out):
    for q in range(NX * NT):
        piece = jnp.concatenate([term[q, z].astype(F32) for z in range(NZ)], axis=0)
        out[q * QUART : (q + 1) * QUART, :] = piece[:COLS, :].T


def place_kernel(r0, r1, r2, r3, out, token):
    token[...] = jnp.zeros(TOKEN.shape, TOKEN.dtype)
    mine, y = 2 * lax.axis_index("xl") + lax.axis_index("xh"), lax.axis_index("y")
    for r, got in enumerate((r0, r1, r2, r3)):
        q = mine ^ r
        for k in range(NY):
            block = y ^ STEPS[k % HALF] ^ (k // HALF)
            at = pl.ds(pl.multiple_of(block * 4 * QUART + q * QUART, QUART), QUART)
            out[:, at] = got[:, k * QUART : (k + 1) * QUART]


def whole(count):
    return [pl.BlockSpec(memory_space=pltpu.VMEM)] * count


UNUSED = [pl.BlockSpec(memory_space=pl.ANY)]
SCALARS = pl.BlockSpec(memory_space=pltpu.SMEM)
PARAMS = pltpu.CompilerParams(vmem_limit_bytes=48 * 1024 * 1024)
LARGE = pltpu.CompilerParams(vmem_limit_bytes=60 * 1024 * 1024)


def per_device(activations, norm_gain, key_weight, key_grad, doc_lengths):
    rows = 128
    blocks, prepared = pl.pallas_call(
        prep_kernel,
        grid=(TOK // rows,),
        in_specs=[
            SCALARS,
            pl.BlockSpec((rows, D), lambda i: (i, 0)),
            pl.BlockSpec((1, D), lambda i: (0, 0)),
            pl.BlockSpec((rows, COLS), lambda i: (i, 0)),
        ],
        out_specs=[
            pl.BlockSpec((4, rows, FEAT + COLS), lambda i: (0, i, 0)),
            pl.BlockSpec(TOKEN.shape, lambda i: (0, 0)),
        ],
        out_shape=[jax.ShapeDtypeStruct((4, TOK, FEAT + COLS), BF16), TOKEN],
        compiler_params=LARGE,
        name="prep",
    )(doc_lengths, activations, norm_gain[None, :], key_grad)

    got = lax.all_to_all(blocks, ("xl", "xh"), 0, 0, tiled=True)

    half_weight = pl.pallas_call(
        half_kernel,
        in_specs=whole(1) + UNUSED,
        out_specs=whole(1)[0],
        out_shape=jax.ShapeDtypeStruct((NT * QUART, COLS), BF16),
        compiler_params=PARAMS,
        name="half_weight",
    )(key_weight, prepared)
    near = jnp.stack(
        [half_weight]
        + [lax.ppermute(half_weight, "y", [(i, i ^ e) for i in range(NY)]) for e in STEPS[1:]]
    )
    far = lax.ppermute(near, "y", [(i, i ^ 1) for i in range(NY)])

    mine = pl.pallas_call(
        pack_kernel,
        grid=(1,),
        in_specs=[pl.BlockSpec((4, TOK, COLS), lambda i: (0, 0, FEAT // COLS))] + UNUSED,
        out_specs=pl.BlockSpec((4, TOK, COLS), lambda i: (0, 0, 0)),
        out_shape=jax.ShapeDtypeStruct((4, TOK, COLS), BF16),
        compiler_params=PARAMS,
        name="pack",
    )(got, near)
    other = lax.ppermute(mine, "t", [(0, 1), (1, 0)])

    term = pl.pallas_call(
        own_kernel,
        in_specs=whole(1),
        out_specs=whole(1)[0],
        out_shape=jax.ShapeDtypeStruct((NY, COLS, QUART), BF16),
        compiler_params=PARAMS,
        name="own_grad",
    )(got)
    term = pl.pallas_call(
        grad_kernel,
        in_specs=whole(3) + UNUSED,
        out_specs=whole(1)[0],
        out_shape=jax.ShapeDtypeStruct((NY, KV, QUART), BF16),
        compiler_params=PARAMS,
        name="weight_grad",
    )(got, other, term, far)

    swapped = pl.pallas_call(
        other_kernel,
        in_specs=whole(3),
        out_specs=whole(1)[0],
        out_shape=jax.ShapeDtypeStruct((4 * TOK + FEAT, COLS), BF16),
        compiler_params=PARAMS,
        name="to_other",
    )(mine, near, far)
    swapped = lax.ppermute(swapped, "t", [(0, 1), (1, 0)])
    shards = pl.BlockSpec((4, TOK, COLS), lambda i: (0, 0, 0))
    *products, multiplied = pl.pallas_call(
        input_kernel,
        grid=(2,),
        in_specs=[shards] * 3 + [pl.BlockSpec((4 * TOK + FEAT, COLS), lambda i: (0, 0))],
        out_specs=[pl.BlockSpec((TOK, FEAT // 2), lambda i: (0, i))] * 4
        + [pl.BlockSpec(TOKEN.shape, lambda i: (0, 0))],
        out_shape=[jax.ShapeDtypeStruct((TOK, FEAT), BF16)] * 4 + [TOKEN],
        compiler_params=PARAMS,
        name="input_grad",
    )(mine, near, far, swapped)

    returned = []
    for r in range(4):
        r0, r1 = r >> 1, r & 1
        pairs = [
            (4 * i + 2 * j + k, 4 * (i ^ r0) + 2 * (k ^ r1) + j)
            for i in range(2)
            for j in range(2)
            for k in range(2)
        ]
        returned.append(lax.ppermute(products[r], ("xl", "xh", "t"), pairs))

    term = lax.all_to_all(term, "y", 0, 0, axis_index_groups=LAST_FIRST, tiled=True)
    term = pl.pallas_call(
        sum_y_kernel,
        in_specs=whole(1) + [pl.BlockSpec(memory_space=pl.ANY)],
        out_specs=whole(1)[0],
        out_shape=jax.ShapeDtypeStruct((NZ, NT, ZCOLS, QUART), BF16),
        compiler_params=PARAMS,
        name="sum_y",
    )(term, multiplied)
    term = lax.all_to_all(term, "z", 0, 0, axis_index_groups=ALONG_Z, tiled=True)
    rows = 64
    normed_grad, placed = pl.pallas_call(
        place_kernel,
        grid=(TOK // rows,),
        in_specs=[pl.BlockSpec((rows, FEAT), lambda i: (i, 0))] * 4,
        out_specs=[
            pl.BlockSpec((rows, 4 * FEAT), lambda i: (i, 0)),
            pl.BlockSpec(TOKEN.shape, lambda i: (0, 0)),
        ],
        out_shape=[jax.ShapeDtypeStruct((TOK, 4 * FEAT), BF16), TOKEN],
        compiler_params=PARAMS,
        name="placed",
    )(*returned)
    pieces = jax.ShapeDtypeStruct((NZ, NT, ZCOLS, QUART), BF16)
    term = pl.pallas_call(
        sum_z_kernel,
        in_specs=whole(1) + [pl.BlockSpec(memory_space=pl.ANY)] * 4,
        out_specs=whole(1)[0],
        out_shape=pieces,
        compiler_params=PARAMS,
        name="sum_z",
    )(term, *returned)
    term = lax.all_to_all(term, "z", 0, 0, axis_index_groups=ALONG_Z, tiled=True)
    term = pl.pallas_call(
        split_kernel,
        in_specs=whole(1) + UNUSED,
        out_specs=whole(1)[0],
        out_shape=jax.ShapeDtypeStruct((NX * NT, NZ, ZCOLS, QUART), BF16),
        compiler_params=PARAMS,
        name="split",
    )(term, placed)
    term = lax.all_to_all(term, ("xl", "t"), 0, 0, tiled=True)
    weight_grad = pl.pallas_call(
        turn_kernel,
        in_specs=whole(1),
        out_specs=whole(1)[0],
        out_shape=jax.ShapeDtypeStruct((NX * NT * QUART, COLS), F32),
        compiler_params=PARAMS,
        name="turn",
    )(term)

    return (weight_grad, normed_grad)


def solution(mesh):
    fine = Mesh(mesh.devices.reshape(NZ, NX, 2, NY, NT), ("z", "xl", "xh", "y", "t"))
    tokens = ("z", "xl", "xh", "y")
    return jax.shard_map(
        per_device,
        mesh=fine,
        in_specs=(
            P(tokens, None),
            P(),
            P(("xh", "y"), "t"),
            P(tokens, "t"),
            P(tokens, None),
        ),
        out_specs=(P(("xh", "y"), "t"), P(tokens, "t")),
        check_vma=False,
    )
```

```python
import functools
import math

import jax
import jax.numpy as jnp
from jax import lax
from jax.experimental import pallas as pl
from jax.experimental.pallas import tpu as pltpu
from jax.sharding import Mesh, PartitionSpec as P

NZ, NX, NY, NT = 12, 2, 8, 2
TOK, D, HS, COLS = 256, 8192, 128, 256
QUART = 128
HALF = NY // 2
STEPS = (0, 6, 2, 4)
TOKEN = jax.ShapeDtypeStruct((8, 128), jnp.float32)
FEAT = NY * QUART
KV = NT * COLS
ALONG_Y = [[3, 2, 1, 7, 6, 0, 5, 4]]
ALONG_Z = [[(7 - p) % NZ for p in range(NZ)]]
ZCOLS = 24
BF16, F32 = jnp.bfloat16, jnp.float32


def prep_kernel(doc, act, gain, key_grad, out, token_out):
    t = lax.axis_index("t")
    token_out[...] = jnp.zeros(TOKEN.shape, TOKEN.dtype)
    rows = act.shape[0]
    token = pl.program_id(0) * rows + lax.broadcasted_iota(jnp.int32, (rows, HS), 0)
    second = doc[0, 0]
    third = second + doc[0, 1]
    fourth = third + doc[0, 2]
    start = jnp.where(
        token >= fourth,
        fourth,
        jnp.where(token >= third, third, jnp.where(token >= second, second, 0)),
    )
    lane = lax.broadcasted_iota(jnp.int32, (rows, HS), 1)
    half = (lane[:1] % (HS // 2)).astype(F32)
    freq = jnp.exp(half * (-2.0 * math.log(1000000.0) / HS))
    angle = (token - start).astype(F32) * freq
    cosine = jnp.cos(angle)
    sine = jnp.sin(angle)
    sine = jnp.where(lane < HS // 2, sine, -sine)
    for h in range(COLS // HS):
        v = key_grad[:, h * HS : (h + 1) * HS].astype(F32)
        v = (v * cosine + pltpu.roll(v, HS // 2, 1) * sine).astype(BF16)
        for i in range(4):
            out[i, :, FEAT + h * HS : FEAT + (h + 1) * HS] = v

    square = jnp.zeros((rows, 128), F32)
    for j in range(D // 128):
        v = act[:, j * 128 : (j + 1) * 128].astype(F32)
        square = square + v * v
    scale = lax.rsqrt(jnp.sum(square, axis=1, keepdims=True) * (1.0 / D) + 1e-06)
    for i in range(4):
        base = (i & 1) * (D // 2) + (2 * (i >> 1) + t) * QUART
        for j in range(NY):
            at = pl.ds(pl.multiple_of(base + j * 4 * QUART, 128), QUART)
            v = act[:, at].astype(F32) * scale * gain[:, at]
            out[i, :, j * QUART : (j + 1) * QUART] = v.astype(BF16)


def half_kernel(weight, after, out):
    del after
    half = NT * QUART
    out[...] = weight[pl.ds(pl.multiple_of(lax.axis_index("xl") * half, half), half), :]


def pack_kernel(got, after, out):
    del after
    out[...] = got[...]


def product(rot, got):
    rot = rot.reshape(4 * TOK, COLS)
    normed = got[:, :, :FEAT].reshape(4 * TOK, FEAT)
    g = lax.dot_general(rot, normed, (((0,), (0,)), ((), ())), preferred_element_type=F32)
    return g.astype(BF16)


def own_kernel(got, out):
    g = product(got[:, :, FEAT:], got)
    for y in range(NY):
        out[y] = g[:, y * QUART : (y + 1) * QUART]


def grad_kernel(got, other, own, after, out):
    del after
    t = lax.axis_index("t")
    mine = pl.ds(pl.multiple_of(t * COLS, COLS), COLS)
    rest = pl.ds(pl.multiple_of((1 - t) * COLS, COLS), COLS)
    g = product(other[...], got)
    for y in range(NY):
        place = ALONG_Y[0].index(y)
        out[place, mine, :] = own[y]
        out[place, rest, :] = g[:, y * QUART : (y + 1) * QUART]


def other_kernel(mine, near, far, out):
    out[: 4 * TOK, :] = mine[...].reshape(4 * TOK, COLS)
    rows = pl.ds(pl.multiple_of((1 - lax.axis_index("t")) * QUART, QUART), QUART)
    for k in range(NY):
        shard = near[k, rows, :] if k < HALF else far[k - HALF, rows, :]
        out[4 * TOK + k * QUART : 4 * TOK + (k + 1) * QUART, :] = shard


def input_kernel(mine, near, far, other, *outs):
    outs, token = outs[:4], outs[4]
    token[...] = jnp.zeros(TOKEN.shape, TOKEN.dtype)
    xl, t = lax.axis_index("xl"), lax.axis_index("t")
    own = pl.ds(pl.multiple_of(t * QUART, QUART), QUART)

    def multiply(weight, h):
        lhs = []
        for r in range(4):
            i = 2 * (xl ^ (r >> 1)) + (t ^ (r & 1))
            rows = pl.ds(pl.multiple_of(i * TOK, TOK), TOK)
            lhs.append(jnp.concatenate([mine[i], other[rows, :]], axis=1))
        lhs = jnp.concatenate(lhs, axis=0)
        for j in range(0, HALF, 2):
            at = 4 * TOK + (HALF * h + j) * QUART
            rhs = jnp.concatenate(
                [
                    jnp.concatenate([weight[j + k, own, :] for k in range(2)], axis=0),
                    other[at : at + 2 * QUART, :],
                ],
                axis=1,
            )
            p = lax.dot_general(lhs, rhs, (((1,), (1,)), ((), ())), preferred_element_type=F32)
            p = p.astype(BF16)
            for r, out in enumerate(outs):
                out[:, j * QUART : (j + 2) * QUART] = p[r * TOK : (r + 1) * TOK, :]

    pl.when(pl.program_id(0) == 0)(functools.partial(multiply, near, 0))
    pl.when(pl.program_id(0) == 1)(functools.partial(multiply, far, 1))


def sum_y_kernel(term, after, out):
    del after
    total = term[0].astype(F32)
    for y in range(1, NY):
        total = total + term[y].astype(F32)
    zero = jnp.zeros((NZ * ZCOLS - COLS, QUART), F32)
    for t in range(NT):
        padded = jnp.concatenate([total[t * COLS : (t + 1) * COLS, :], zero], axis=0)
        for z in range(NZ):
            out[z, t] = padded[z * ZCOLS : (z + 1) * ZCOLS, :].astype(BF16)


def sum_z_kernel(term, after0, after1, after2, after3, out):
    del after0, after1, after2, after3
    for t in range(NT):
        total = term[0, t].astype(F32)
        for z in range(1, NZ):
            total = total + term[z, t].astype(F32)
        total = (total * (1.0 / (NZ * NX))).astype(BF16)
        for z in range(NZ):
            out[z, t] = total


def split_kernel(term, after, out):
    del after
    for z in range(NZ):
        for t in range(NT):
            for xl in range(NX):
                out[NT * xl + t, z] = term[z, t]


def turn_kernel(term, out):
    for q in range(NX * NT):
        piece = jnp.concatenate([term[q, z].astype(F32) for z in range(NZ)], axis=0)
        out[q * QUART : (q + 1) * QUART, :] = piece[:COLS, :].T


def place_kernel(r0, r1, r2, r3, out, token):
    token[...] = jnp.zeros(TOKEN.shape, TOKEN.dtype)
    mine, y = 2 * lax.axis_index("xl") + lax.axis_index("xh"), lax.axis_index("y")
    for r, got in enumerate((r0, r1, r2, r3)):
        q = mine ^ r
        for k in range(NY):
            block = y ^ STEPS[k % HALF] ^ (k // HALF)
            at = pl.ds(pl.multiple_of(block * 4 * QUART + q * QUART, QUART), QUART)
            out[:, at] = got[:, k * QUART : (k + 1) * QUART]


def whole(count):
    return [pl.BlockSpec(memory_space=pltpu.VMEM)] * count


UNUSED = [pl.BlockSpec(memory_space=pl.ANY)]
SCALARS = pl.BlockSpec(memory_space=pltpu.SMEM)
PARAMS = pltpu.CompilerParams(vmem_limit_bytes=48 * 1024 * 1024)
LARGE = pltpu.CompilerParams(vmem_limit_bytes=60 * 1024 * 1024)


def per_device(activations, norm_gain, key_weight, key_grad, doc_lengths):
    rows = 128
    blocks, prepared = pl.pallas_call(
        prep_kernel,
        grid=(TOK // rows,),
        in_specs=[
            SCALARS,
            pl.BlockSpec((rows, D), lambda i: (i, 0)),
            pl.BlockSpec((1, D), lambda i: (0, 0)),
            pl.BlockSpec((rows, COLS), lambda i: (i, 0)),
        ],
        out_specs=[
            pl.BlockSpec((4, rows, FEAT + COLS), lambda i: (0, i, 0)),
            pl.BlockSpec(TOKEN.shape, lambda i: (0, 0)),
        ],
        out_shape=[jax.ShapeDtypeStruct((4, TOK, FEAT + COLS), BF16), TOKEN],
        compiler_params=LARGE,
        name="prep",
    )(doc_lengths, activations, norm_gain[None, :], key_grad)

    got = lax.all_to_all(blocks, ("xl", "xh"), 0, 0, tiled=True)

    half_weight = pl.pallas_call(
        half_kernel,
        in_specs=whole(1) + UNUSED,
        out_specs=whole(1)[0],
        out_shape=jax.ShapeDtypeStruct((NT * QUART, COLS), BF16),
        compiler_params=PARAMS,
        name="half_weight",
    )(key_weight, prepared)
    near = jnp.stack(
        [half_weight]
        + [lax.ppermute(half_weight, "y", [(i, i ^ e) for i in range(NY)]) for e in STEPS[1:]]
    )
    far = lax.ppermute(near, "y", [(i, i ^ 1) for i in range(NY)])

    mine = pl.pallas_call(
        pack_kernel,
        grid=(1,),
        in_specs=[pl.BlockSpec((4, TOK, COLS), lambda i: (0, 0, FEAT // COLS))] + UNUSED,
        out_specs=pl.BlockSpec((4, TOK, COLS), lambda i: (0, 0, 0)),
        out_shape=jax.ShapeDtypeStruct((4, TOK, COLS), BF16),
        compiler_params=PARAMS,
        name="pack",
    )(got, near)
    other = lax.ppermute(mine, "t", [(0, 1), (1, 0)])

    term = pl.pallas_call(
        own_kernel,
        in_specs=whole(1),
        out_specs=whole(1)[0],
        out_shape=jax.ShapeDtypeStruct((NY, COLS, QUART), BF16),
        compiler_params=PARAMS,
        name="own_grad",
    )(got)
    term = pl.pallas_call(
        grad_kernel,
        in_specs=whole(3) + UNUSED,
        out_specs=whole(1)[0],
        out_shape=jax.ShapeDtypeStruct((NY, KV, QUART), BF16),
        compiler_params=PARAMS,
        name="weight_grad",
    )(got, other, term, far)

    swapped = pl.pallas_call(
        other_kernel,
        in_specs=whole(3),
        out_specs=whole(1)[0],
        out_shape=jax.ShapeDtypeStruct((4 * TOK + FEAT, COLS), BF16),
        compiler_params=PARAMS,
        name="to_other",
    )(mine, near, far)
    swapped = lax.ppermute(swapped, "t", [(0, 1), (1, 0)])
    shards = pl.BlockSpec((4, TOK, COLS), lambda i: (0, 0, 0))
    *products, multiplied = pl.pallas_call(
        input_kernel,
        grid=(2,),
        in_specs=[shards] * 3 + [pl.BlockSpec((4 * TOK + FEAT, COLS), lambda i: (0, 0))],
        out_specs=[pl.BlockSpec((TOK, FEAT // 2), lambda i: (0, i))] * 4
        + [pl.BlockSpec(TOKEN.shape, lambda i: (0, 0))],
        out_shape=[jax.ShapeDtypeStruct((TOK, FEAT), BF16)] * 4 + [TOKEN],
        compiler_params=PARAMS,
        name="input_grad",
    )(mine, near, far, swapped)

    returned = []
    for r in range(4):
        r0, r1 = r >> 1, r & 1
        pairs = [
            (4 * i + 2 * j + k, 4 * (i ^ r0) + 2 * (k ^ r1) + j)
            for i in range(2)
            for j in range(2)
            for k in range(2)
        ]
        returned.append(lax.ppermute(products[r], ("xl", "xh", "t"), pairs))

    term = lax.all_to_all(term, "y", 0, 0, axis_index_groups=ALONG_Y, tiled=True)
    term = pl.pallas_call(
        sum_y_kernel,
        in_specs=whole(1) + [pl.BlockSpec(memory_space=pl.ANY)],
        out_specs=whole(1)[0],
        out_shape=jax.ShapeDtypeStruct((NZ, NT, ZCOLS, QUART), BF16),
        compiler_params=PARAMS,
        name="sum_y",
    )(term, multiplied)
    term = lax.all_to_all(term, "z", 0, 0, axis_index_groups=ALONG_Z, tiled=True)
    rows = 64
    normed_grad, placed = pl.pallas_call(
        place_kernel,
        grid=(TOK // rows,),
        in_specs=[pl.BlockSpec((rows, FEAT), lambda i: (i, 0))] * 4,
        out_specs=[
            pl.BlockSpec((rows, 4 * FEAT), lambda i: (i, 0)),
            pl.BlockSpec(TOKEN.shape, lambda i: (0, 0)),
        ],
        out_shape=[jax.ShapeDtypeStruct((TOK, 4 * FEAT), BF16), TOKEN],
        compiler_params=PARAMS,
        name="placed",
    )(*returned)
    pieces = jax.ShapeDtypeStruct((NZ, NT, ZCOLS, QUART), BF16)
    term = pl.pallas_call(
        sum_z_kernel,
        in_specs=whole(1) + [pl.BlockSpec(memory_space=pl.ANY)] * 4,
        out_specs=whole(1)[0],
        out_shape=pieces,
        compiler_params=PARAMS,
        name="sum_z",
    )(term, *returned)
    term = lax.all_to_all(term, "z", 0, 0, axis_index_groups=ALONG_Z, tiled=True)
    term = pl.pallas_call(
        split_kernel,
        in_specs=whole(1) + UNUSED,
        out_specs=whole(1)[0],
        out_shape=jax.ShapeDtypeStruct((NX * NT, NZ, ZCOLS, QUART), BF16),
        compiler_params=PARAMS,
        name="split",
    )(term, placed)
    term = lax.all_to_all(term, ("xl", "t"), 0, 0, tiled=True)
    weight_grad = pl.pallas_call(
        turn_kernel,
        in_specs=whole(1),
        out_specs=whole(1)[0],
        out_shape=jax.ShapeDtypeStruct((NX * NT * QUART, COLS), F32),
        compiler_params=PARAMS,
        name="turn",
    )(term)

    return (weight_grad, normed_grad)


def solution(mesh):
    fine = Mesh(mesh.devices.reshape(NZ, NX, 2, NY, NT), ("z", "xl", "xh", "y", "t"))
    tokens = ("z", "xl", "xh", "y")
    return jax.shard_map(
        per_device,
        mesh=fine,
        in_specs=(
            P(tokens, None),
            P(),
            P(("xh", "y"), "t"),
            P(tokens, "t"),
            P(tokens, None),
        ),
        out_specs=(P(("xh", "y"), "t"), P(tokens, "t")),
        check_vma=False,
    )
```
